128 devices in a mesh: strip: 128 (over z, y, x, core).
Axes of the slice: x: 4, y: 4, z: 4, core: 2. Of those that a mesh axis runs over, the one named last changes fastest.
Arguments:
- density: float32 [65536, 64], P('strip'), may hold values from -6 to 6
- near_blocks: float32 [65536, 6144], P('strip'), may hold values from -0.078125 to 0.078125
- u_far: bfloat16 [65536, 128, 32], P('strip'), may hold values from -0.09375 to 0.09375
- v_far: bfloat16 [65536, 128, 32], P('strip'), may hold values from -0.25 to 0.25
- ranks: int32 [128, 128], replicated, may hold values from 0 to 32, as said below
- near_list: int32 [128, 12], replicated, may hold values from 0 to 127, as said below
- near_count: int32 [128], replicated, may hold values from 6 to 12, as said below
Outputs:
- potential: float32 [65536, 64], P('strip')
The draws below stay inside these ranges and needn't reach their ends.
Inputs may be any that keep to these rules, and one draw needn't show every extreme that they name: near_list row i holds i first, then near_count[i] - 1 distinct other strips j with |j - i| <= 8; its remaining entries repeat i. `near_count`: both ends are reached. ranks[i, j] is 0 exactly when j is among the first near_count[i] entries of near_list row i, otherwise from 8 to 32; 32 is reached.
All inputs are finite; a program needn't handle non-finite values.
Results may differ from the reference program's by a relative error of at most 0.0027.
Values may be sent and summed in bfloat16 or wider, within the bound.
No kernel may reach another device: no remote copies, remote signals or barrier semaphores. Data moves between devices by JAX's collectives and lax.ppermute only.
A program may use at most 128 MiB of HBM per device.

```python
import jax
import jax.numpy as jnp
import numpy as np
from jax import lax

STRIP_ROWS = 512
RHS = 64
RANK_MAX = 32
NEAR_MAX = 12
WINDOW = 8
STRIPS = 128
ORDER = 65536


def near_tables(key):
    offsets = np.array([shift_value for shift_value in range(-WINDOW, WINDOW + 1) if shift_value != 0], dtype=np.int32)
    spread = offsets.shape[0]
    strip_index = jnp.arange(STRIPS, dtype=jnp.int32)
    candidates = strip_index[:, None] + jnp.asarray(offsets)[None, :]
    inside = (candidates >= 0) & (candidates < STRIPS)
    score_key, count_key = jax.random.split(key)
    scores = jax.random.randint(score_key, (STRIPS, spread), 0, 1 << 20) * spread + jnp.arange(spread, dtype=jnp.int32)[None, :]
    scores = jnp.where(inside, scores, -1)
    ordering = jnp.argsort(-scores, axis=1, stable=True)
    ranked = jnp.take_along_axis(candidates, ordering, axis=1)
    available = jnp.sum(inside.astype(jnp.int32), axis=1)
    counts = jax.random.randint(count_key, (STRIPS,), 6, NEAR_MAX + 1)
    counts = jnp.minimum(counts, available + 1)
    counts = counts.at[STRIPS // 4].set(NEAR_MAX).at[STRIPS // 4 + 1].set(6)
    slot_index = jnp.arange(1, NEAR_MAX, dtype=jnp.int32)
    others = jnp.where(slot_index[None, :] < counts[:, None], ranked[:, :NEAR_MAX - 1], strip_index[:, None])
    tables = jnp.concatenate([strip_index[:, None], others], axis=1)
    return (tables.astype(jnp.int32), counts.astype(jnp.int32))


def draw_near_list(key, part):
    tables, counts = near_tables(key)
    return tables


def draw_near_count(key, part):
    tables, counts = near_tables(key)
    return counts


def draw_ranks(key, part):
    tables, counts = near_tables(key)
    key = jax.random.fold_in(key, 7)
    values = jax.random.randint(key, (STRIPS, STRIPS), 8, RANK_MAX + 1)
    values = values.at[0, STRIPS // 2].set(RANK_MAX)
    live = jnp.arange(NEAR_MAX, dtype=jnp.int32)[None, :] < counts[:, None]
    columns = jnp.arange(STRIPS, dtype=jnp.int32)
    nearby = jnp.any((tables[:, :, None] == columns[None, None, :]) & live[:, :, None], axis=1)
    return jnp.where(nearby, 0, values).astype(jnp.int32)


def block_scale(own_key, shape, pieces, low, top_value):
    def one(dim, blocks):
        draws = jax.random.uniform(jax.random.fold_in(jax.random.fold_in(own_key, 6), dim), (blocks,), jnp.float32, low / len(pieces), top_value / len(pieces))
        return jnp.repeat(jnp.exp(draws), shape[dim] // blocks).reshape((-1,) + (1,) * (len(shape) - dim - 1))

    level = one(*pieces[0])
    for cut in pieces[1:]:
        level = level * one(*cut)
    return level


def scatter_about(stream_key, extent, width, bound, cuts=(), kind=jnp.bfloat16):
    drawn = width * jax.random.normal(stream_key, extent, jnp.float32)
    if cuts:
        drawn = drawn * block_scale(stream_key, extent, cuts, -0.22, 0.18)
    return jnp.clip(drawn, -bound, bound).astype(kind)


def setup_inputs(seed: int = 0) -> dict:
    key_of = jax.random.split(jax.random.key(seed), 8)
    return {
        "density": scatter_about(key_of[0], (ORDER, RHS), 1.0, 6.0, ((0, 128),), jnp.float32),
        "near_blocks": scatter_about(key_of[1], (ORDER, NEAR_MAX * STRIP_ROWS), (NEAR_MAX * STRIP_ROWS) ** -0.5, 0.078125, ((0, 128),), jnp.float32),
        "u_far": scatter_about(key_of[2], (ORDER, STRIPS, RANK_MAX), (STRIPS * RANK_MAX) ** -0.5, 0.09375, ((0, 128),)),
        "v_far": scatter_about(key_of[3], (ORDER, STRIPS, RANK_MAX), STRIP_ROWS ** -0.5, 0.25, ((0, 128),)),
        "ranks": draw_ranks(jax.random.fold_in(key_of[7], 71), 0),
        "near_list": draw_near_list(jax.random.fold_in(key_of[7], 71), 0),
        "near_count": draw_near_count(jax.random.fold_in(key_of[7], 71), 0),
    }


def reference(density, near_blocks, u_far, v_far, ranks, near_list, near_count):
    source_bf = lax.optimization_barrier(density.astype(jnp.bfloat16))
    source_blocks = source_bf.reshape(STRIPS, STRIP_ROWS, RHS)
    v_blocks = v_far.reshape(STRIPS, STRIP_ROWS, STRIPS, RANK_MAX)

    def project(operands):
        v_one, x_one, rank_column = operands
        product = jnp.einsum('mik,mr->ikr', v_one.astype(jnp.float32), x_one.astype(jnp.float32))
        keep = jnp.arange(RANK_MAX, dtype=jnp.int32)[None, :] < rank_column[:, None]
        return jnp.where(keep[:, :, None], product, 0.0).astype(jnp.bfloat16)

    coefficients = lax.map(project, (v_blocks, source_blocks, ranks.T))
    by_row = jnp.transpose(coefficients, (1, 0, 2, 3)).reshape(STRIPS, STRIPS * RANK_MAX, RHS)
    u_blocks = u_far.reshape(STRIPS, STRIP_ROWS, STRIPS * RANK_MAX)

    def far_rows(operands):
        return jnp.dot(operands[0], operands[1], preferred_element_type=jnp.float32)

    far_field = lax.map(far_rows, (u_blocks, by_row))
    dense_blocks = density.reshape(STRIPS, STRIP_ROWS, RHS)
    near_rows = near_blocks.reshape(STRIPS, STRIP_ROWS, NEAR_MAX * STRIP_ROWS)

    def near_one(operands):
        block, picks, count = operands
        live = jnp.arange(NEAR_MAX, dtype=jnp.int32) < count
        gathered = jnp.where(live[:, None, None], dense_blocks[picks], 0.0)
        return jnp.dot(block, gathered.reshape(NEAR_MAX * STRIP_ROWS, RHS),
                       precision=lax.Precision.HIGHEST, preferred_element_type=jnp.float32)

    near_field = lax.map(near_one, (near_rows, near_list, near_count))
    return (near_field + far_field).reshape(ORDER, RHS)
```

```python
import functools

import jax
import jax.numpy as jnp
from jax import lax
from jax.experimental import pallas as pl
from jax.experimental.pallas import tpu as pltpu
from jax.sharding import PartitionSpec as P

WINDOW = 8
REACH = WINDOW // 2

bf16 = jnp.bfloat16
f32 = jnp.float32
MiB = 2**20


def project_kernel(chunk, me_ref, x_ref, ranks_ref, v_ref, out_ref, raw_ref, turned_ref, sems):
    rows, rank_max, strips = raw_ref.shape
    parts = rows // chunk
    copies = [
        pltpu.make_async_copy(
            v_ref.at[pl.ds(n * chunk, chunk)], raw_ref.at[pl.ds(n * chunk, chunk)], sems.at[n]
        )
        for n in range(parts)
    ]
    for copy in copies:
        copy.start()
    source = x_ref[...].astype(bf16)
    hot = (lax.broadcasted_iota(jnp.int32, (8, strips), 1) == me_ref[0]).astype(bf16)
    rank = lax.dot_general(
        hot,
        ranks_ref[...].astype(f32).astype(bf16),
        (((1,), (1,)), ((), ())),
        preferred_element_type=f32,
    )
    rank = jnp.broadcast_to(rank[:1], (source.shape[0], strips))
    for n in range(parts):
        copies[n].wait()
        turned_ref[:, pl.ds(n * chunk, chunk), :] = jnp.swapaxes(
            raw_ref[pl.ds(n * chunk, chunk)], 0, 1
        )
    factors = jnp.concatenate([turned_ref[k] for k in range(rank_max)], axis=1)
    product = jnp.dot(source, factors, preferred_element_type=f32)
    kept = [
        jnp.where(rank > k, product[:, k * strips : (k + 1) * strips], 0.0).astype(bf16)
        for k in range(rank_max)
    ]
    pairs = [jnp.concatenate(kept[k : k + 2], axis=0).T for k in range(0, rank_max, 2)]
    out_ref[...] = jnp.swapaxes(jnp.stack(pairs), 0, 1)


def project(me, source, ranks, v_turned):
    rows, rank_max, strips = v_turned.shape
    sides = source.shape[0]
    chunk = 64
    return pl.pallas_call(
        functools.partial(project_kernel, chunk),
        in_specs=[
            pl.BlockSpec(memory_space=pltpu.SMEM),
            pl.BlockSpec(memory_space=pltpu.VMEM),
            pl.BlockSpec(memory_space=pltpu.VMEM),
            pl.BlockSpec(memory_space=pl.ANY),
        ],
        out_specs=pl.BlockSpec(memory_space=pltpu.VMEM),
        out_shape=jax.ShapeDtypeStruct((strips, rank_max // 2, 2 * sides), bf16),
        scratch_shapes=[
            pltpu.VMEM((rows, rank_max, strips), bf16),
            pltpu.VMEM((rank_max, rows, strips), bf16),
            pltpu.SemaphoreType.DMA((rows // chunk,)),
        ],
        compiler_params=pltpu.CompilerParams(vmem_limit_bytes=28 * MiB),
        cost_estimate=pl.CostEstimate(
            flops=2 * rows * rank_max * strips * sides,
            bytes_accessed=2 * rows * rank_max * strips,
            transcendentals=0,
        ),
        name="project",
    )(me, source, ranks, v_turned)


def near_kernel(me_ref, list_ref, count_ref, blocks_ref, pair_ref, *refs):
    direct, swapped, (out_ref, table_ref, tiles_ref, sems) = (
        refs[:REACH],
        refs[REACH : 2 * REACH],
        refs[2 * REACH :],
    )
    slots = list_ref.shape[0]
    rows = tiles_ref.shape[1]
    me = me_ref[0]
    core = me % 2
    copies = [
        pltpu.make_async_copy(
            blocks_ref.at[:, pl.ds(s * rows, rows)], tiles_ref.at[s], sems.at[s]
        )
        for s in range(slots)
    ]
    for copy in copies:
        copy.start()
    for n, ref in enumerate((pair_ref, *direct, *swapped)):
        table_ref[pl.ds(2 * n, 2)] = ref[...]
    total = jnp.zeros(out_ref.shape, f32)
    for s in range(slots):
        strip = list_ref[s, me]
        live = s < count_ref[me]
        chips = strip // 2 - me // 2
        distance = jnp.abs(chips)
        is_own = distance == 0
        is_direct = (chips > 0) == (core == 0)
        sender_core = jnp.where(jnp.logical_or(is_own, is_direct), core, 1 - core)
        group = jnp.where(is_own, 0, distance + jnp.where(is_direct, 0, REACH))
        place = jnp.clip(2 * group + jnp.where(strip % 2 == sender_core, 0, 1), 0, table_ref.shape[0] - 1)
        strip_density = table_ref[place]
        strip_density = jnp.where(live, strip_density, jnp.zeros_like(strip_density))
        copies[s].wait()
        tile = tiles_ref[s]
        high = tile.astype(bf16)
        low = (tile - high.astype(f32)).astype(bf16)
        for piece in (high, low):
            total += lax.dot_general(
                strip_density, piece, (((1,), (1,)), ((), ())), preferred_element_type=f32
            )
    out_ref[...] = total


def near(me, near_list, near_count, near_blocks, pair, direct, swapped):
    rows = near_blocks.shape[0]
    slots = near_list.shape[1]
    sides = pair.shape[1]
    smem = pl.BlockSpec(memory_space=pltpu.SMEM)
    vmem = pl.BlockSpec(memory_space=pltpu.VMEM)
    return pl.pallas_call(
        near_kernel,
        in_specs=[smem, smem, smem, pl.BlockSpec(memory_space=pl.ANY)] + [vmem] * (1 + 2 * REACH),
        out_specs=vmem,
        out_shape=jax.ShapeDtypeStruct((sides, rows), f32),
        scratch_shapes=[
            pltpu.VMEM((2 + 4 * REACH, sides, rows), bf16),
            pltpu.VMEM((slots, rows, rows), f32),
            pltpu.SemaphoreType.DMA((slots,)),
        ],
        compiler_params=pltpu.CompilerParams(vmem_limit_bytes=32 * MiB),
        cost_estimate=pl.CostEstimate(
            flops=4 * rows * rows * slots * sides,
            bytes_accessed=4 * rows * rows * slots,
            transcendentals=0,
        ),
        name="near",
    )(me, near_list.T, near_count, near_blocks, pair, *direct, *swapped)


def far_kernel(chunk, near_ref, u_ref, coefficients_ref, out_ref, raw_ref, turned_ref, sems):
    rows, rank_max, strips = raw_ref.shape
    sides = out_ref.shape[0]
    parts = rows // chunk
    copies = [
        pltpu.make_async_copy(
            u_ref.at[pl.ds(n * chunk, chunk)], raw_ref.at[pl.ds(n * chunk, chunk)], sems.at[n]
        )
        for n in range(parts)
    ]
    for copy in copies:
        copy.start()
    turned = jnp.swapaxes(coefficients_ref[...], 0, 1)
    weights = jnp.concatenate(
        [
            turned[p][:, half * sides : (half + 1) * sides]
            for p in range(rank_max // 2)
            for half in range(2)
        ],
        axis=0,
    )
    for n in range(parts):
        copies[n].wait()
        turned_ref[:, pl.ds(n * chunk, chunk), :] = jnp.swapaxes(
            raw_ref[pl.ds(n * chunk, chunk)], 0, 1
        )
    factors = jnp.concatenate([turned_ref[k] for k in range(rank_max)], axis=1)
    far = jnp.dot(factors, weights, preferred_element_type=f32)
    out_ref[...] = near_ref[...] + far.T


def add_far(near_field, u_turned, coefficients):
    rows, rank_max, strips = u_turned.shape
    sides = near_field.shape[0]
    chunk = 64
    vmem = pl.BlockSpec(memory_space=pltpu.VMEM)
    return pl.pallas_call(
        functools.partial(far_kernel, chunk),
        in_specs=[vmem, pl.BlockSpec(memory_space=pl.ANY), vmem],
        out_specs=vmem,
        out_shape=jax.ShapeDtypeStruct((sides, rows), f32),
        scratch_shapes=[
            pltpu.VMEM((rows, rank_max, strips), bf16),
            pltpu.VMEM((rank_max, rows, strips), bf16),
            pltpu.SemaphoreType.DMA((rows // chunk,)),
        ],
        compiler_params=pltpu.CompilerParams(vmem_limit_bytes=28 * MiB),
        cost_estimate=pl.CostEstimate(
            flops=2 * rows * rank_max * strips * sides,
            bytes_accessed=2 * rows * rank_max * strips,
            transcendentals=0,
        ),
        name="add_far",
    )(near_field, u_turned, coefficients)


def body(density, near_blocks, u_far, v_far, ranks, near_list, near_count):
    strips = lax.axis_size("strip")
    pairs = strips // 2
    me = lax.axis_index("strip").astype(jnp.int32).reshape(1)
    source = density.T
    swap = [(d, d ^ 1) for d in range(strips)]
    sibling = lax.ppermute(source, "strip", swap)
    outgoing = project(me, source, ranks, jnp.transpose(v_far, (0, 2, 1)))
    source, sibling, outgoing = lax.optimization_barrier((source, sibling, outgoing))
    incoming = lax.all_to_all(outgoing, "strip", split_axis=0, concat_axis=0, tiled=True)
    pair = jnp.stack([source.astype(bf16), sibling.astype(bf16)])
    direct = []
    swapped = []
    for step in range(1, REACH + 1):
        moves = [(2 * (c + step), 2 * c) for c in range(pairs - step)]
        moves += [(2 * c + 1, 2 * (c + step) + 1) for c in range(pairs - step)]
        direct.append(lax.ppermute(pair, "strip", moves))
    for block in direct:
        swapped.append(lax.ppermute(block, "strip", swap))
    near_field = near(me, near_list, near_count, near_blocks, pair, direct, swapped)
    return add_far(near_field, jnp.transpose(u_far, (0, 2, 1)), incoming).T


def solution(mesh):
    return jax.shard_map(
        body,
        mesh=mesh,
        in_specs=(
            P("strip", None),
            P("strip", None),
            P("strip", None, None),
            P("strip", None, None),
            P(),
            P(),
            P(),
        ),
        out_specs=P("strip", None),
        check_vma=False,
    )
```

```python
import jax
import jax.numpy as jnp
from jax import lax
from jax.experimental import pallas as pl
from jax.experimental.pallas import tpu as pltpu
from jax.sharding import PartitionSpec as P

GROUP = 6

bf16 = jnp.bfloat16
f32 = jnp.float32
MiB = 2**20

SMEM = pl.BlockSpec(memory_space=pltpu.SMEM)
VMEM = pl.BlockSpec(memory_space=pltpu.VMEM)
HBM = pl.BlockSpec(memory_space=pltpu.HBM)


def start_all(copies):
    for copy in copies:
        copy.start()


def project_kernel(x_hbm, v_hbm, out_ref, source_ref, x_ref, raw_ref, turned_ref, small, sems):
    rank_max, rows, strips = turned_ref.shape
    sides = source_ref.shape[0]
    parts, pieces = sems.shape
    half = rank_max // parts
    chunk = rows // pieces
    first = pltpu.make_async_copy(x_hbm, x_ref, small)
    copies = [
        [
            pltpu.make_async_copy(
                v_hbm.at[pl.ds(n * chunk, chunk), pl.ds(h * half, half)],
                raw_ref.at[h, pl.ds(n * chunk, chunk)],
                sems.at[h, n],
            )
            for n in range(pieces)
        ]
        for h in range(parts)
    ]
    first.start()
    for part in copies:
        start_all(part)
    first.wait()
    source = x_ref[...].astype(bf16)
    source_ref[...] = source
    for h, part in enumerate(copies):
        for n, copy in enumerate(part):
            copy.wait()
            turned_ref[pl.ds(h * half, half), pl.ds(n * chunk, chunk), :] = jnp.swapaxes(
                raw_ref[h, pl.ds(n * chunk, chunk)], 0, 1
            )
        factors = jnp.concatenate([turned_ref[h * half + k] for k in range(half)], axis=1)
        product = jnp.dot(source, factors, preferred_element_type=f32)
        for k in range(half):
            place = pl.ds(k % 2 * sides, sides)
            value = product[:, k * strips : (k + 1) * strips]
            out_ref[(h * half + k) // 2, place, :] = value.astype(bf16)


def project(source, v_far):
    rows, rank_max, strips = v_far.shape
    sides = source.shape[0]
    parts = 2
    return pl.pallas_call(
        project_kernel,
        in_specs=[HBM, HBM],
        out_specs=[VMEM, VMEM],
        out_shape=[
            jax.ShapeDtypeStruct((rank_max // 2, 2 * sides, strips), bf16),
            jax.ShapeDtypeStruct(source.shape, bf16),
        ],
        scratch_shapes=[
            pltpu.VMEM(source.shape, f32),
            pltpu.VMEM((parts, rows, rank_max // parts, strips), bf16),
            pltpu.VMEM((rank_max, rows, strips), bf16),
            pltpu.SemaphoreType.DMA(()),
            pltpu.SemaphoreType.DMA((parts, 2)),
        ],
        compiler_params=pltpu.CompilerParams(vmem_limit_bytes=50 * MiB),
        cost_estimate=pl.CostEstimate(
            flops=2 * rows * rank_max * strips * sides,
            bytes_accessed=2 * rows * rank_max * strips,
            transcendentals=0,
        ),
        name="project",
    )(source, v_far)


def order_kernel(raw_ref, out_ref):
    turned = jnp.stack([raw_ref[p].T for p in range(raw_ref.shape[0])])
    out_ref[...] = jnp.swapaxes(turned, 0, 1)


def order(raw):
    pairs, width, strips = raw.shape
    return pl.pallas_call(
        order_kernel,
        in_specs=[VMEM],
        out_specs=VMEM,
        out_shape=jax.ShapeDtypeStruct((strips, pairs, width), bf16),
        compiler_params=pltpu.CompilerParams(vmem_limit_bytes=4 * MiB),
        cost_estimate=pl.CostEstimate(
            flops=0, bytes_accessed=4 * pairs * width * strips, transcendentals=0
        ),
        name="order",
    )(raw)


def group_kernel(me_ref, own_ref, sibling_ref, first_ref, second_ref, other_first_ref, other_second_ref, out_ref):
    core = me_ref[0] % 2
    out_ref[2 + core] = own_ref[...]
    out_ref[3 - core] = sibling_ref[...].astype(bf16)
    out_ref[4 - 3 * core] = first_ref[...].astype(bf16)
    out_ref[1 + 3 * core] = other_first_ref[...].astype(bf16)
    out_ref[5 * core] = second_ref[...].astype(bf16)
    out_ref[5 - 5 * core] = other_second_ref[...].astype(bf16)


def group(me, own, *others):
    return pl.pallas_call(
        group_kernel,
        in_specs=[SMEM] + [VMEM] * 6,
        out_specs=VMEM,
        out_shape=jax.ShapeDtypeStruct((GROUP, *own.shape), bf16),
        compiler_params=pltpu.CompilerParams(vmem_limit_bytes=4 * MiB),
        name="group",
    )(me, own, *others)


def near_kernel(me_ref, list_ref, count_ref, blocks_hbm, ranks_ref, own_ref, direct_ref, swapped_ref, out_ref, rank_ref, table_ref, gathered_ref, tiles_ref, sems):
    slots = list_ref.shape[0]
    parts, chunk, columns = tiles_ref.shape
    rows = columns // slots
    copies = [
        pltpu.make_async_copy(blocks_hbm.at[pl.ds(n * chunk, chunk)], tiles_ref.at[n], sems.at[n])
        for n in range(parts)
    ]
    start_all(copies)
    me = me_ref[0]
    core = me % 2
    strips, width = rank_ref.shape
    hot = (lax.broadcasted_iota(jnp.int32, (strips, width), 0) == me).astype(bf16)
    rank = lax.dot_general(
        ranks_ref[...].astype(f32).astype(bf16),
        hot,
        (((0,), (0,)), ((), ())),
        preferred_element_type=f32,
    )
    odd = lax.broadcasted_iota(jnp.int32, (strips, width), 1) >= out_ref.shape[0]
    rank_ref[...] = (rank - odd.astype(f32)).astype(bf16)
    table_ref[pl.ds(GROUP, GROUP)] = own_ref[...]
    table_ref[pl.ds(2 * GROUP * (1 - core), GROUP)] = direct_ref[...]
    table_ref[pl.ds(2 * GROUP * core, GROUP)] = swapped_ref[...]
    pair = me // 2
    above = jnp.where(pair == list_ref.shape[1] // 2 - 3, pair + 1, pair + 3)
    below = jnp.where(pair == 2, 1, pair - 3)
    for s in range(slots):
        strip = list_ref[s, me]
        side = strip // 2 - pair
        middle = jnp.where(side > 1, above, jnp.where(side < -1, below, pair))
        start = jnp.where(side > 1, 2 * GROUP, jnp.where(side < -1, 0, GROUP))
        place = start + jnp.clip(strip - 2 * (middle - 1), 0, GROUP - 1)
        value = table_ref[place]
        value = jnp.where(s < count_ref[me], value, jnp.zeros_like(value))
        gathered_ref[pl.ds(s * rows, rows), :] = value.T
    for n in range(parts):
        copies[n].wait()
        total = jnp.zeros((2 * chunk, out_ref.shape[0]), f32)
        for s in range(slots):
            tile = tiles_ref[n, :, pl.ds(s * rows, rows)]
            high = tile.astype(bf16)
            low = (tile - high.astype(f32)).astype(bf16)
            total += jnp.dot(
                jnp.concatenate([high, low], axis=0),
                gathered_ref[pl.ds(s * rows, rows), :],
                preferred_element_type=f32,
            )
        out_ref[:, pl.ds(n * chunk, chunk)] = (total[:chunk] + total[chunk:]).T


def near(me, near_list, near_count, near_blocks, ranks, own, direct, swapped):
    rows, columns = near_blocks.shape
    sides = own.shape[1]
    parts = 4
    return pl.pallas_call(
        near_kernel,
        in_specs=[SMEM, SMEM, SMEM, HBM, VMEM, VMEM, VMEM, VMEM],
        out_specs=[VMEM, VMEM],
        out_shape=[
            jax.ShapeDtypeStruct((sides, rows), f32),
            jax.ShapeDtypeStruct((ranks.shape[0], 2 * sides), bf16),
        ],
        scratch_shapes=[
            pltpu.VMEM((3 * GROUP, sides, rows), bf16),
            pltpu.VMEM((columns, sides), bf16),
            pltpu.VMEM((parts, rows // parts, columns), f32),
            pltpu.SemaphoreType.DMA((parts,)),
        ],
        compiler_params=pltpu.CompilerParams(vmem_limit_bytes=52 * MiB),
        cost_estimate=pl.CostEstimate(
            flops=4 * rows * columns * sides,
            bytes_accessed=4 * rows * columns,
            transcendentals=0,
        ),
        name="near",
    )(me, near_list.T, near_count, near_blocks, ranks, own, direct, swapped)


def far_kernel(near_ref, rank_ref, u_ref, coefficients_ref, out_ref, turned_ref):
    rows, rank_max, strips = u_ref.shape
    sides = out_ref.shape[0]
    turned_ref[...] = jnp.swapaxes(u_ref[...], 0, 1)
    rank = rank_ref[...]
    turned = jnp.swapaxes(coefficients_ref[...], 0, 1)
    weights = []
    for p in range(rank_max // 2):
        kept = jnp.where(rank > 2 * p, turned[p], jnp.zeros_like(turned[p]))
        weights += [kept[:, :sides], kept[:, sides:]]
    weights = jnp.concatenate(weights, axis=0)
    factors = jnp.concatenate([turned_ref[k] for k in range(rank_max)], axis=1)
    far = jnp.dot(factors, weights, preferred_element_type=f32)
    out_ref[...] = near_ref[...] + far.T


def add_far(near_field, rank, u_far, coefficients):
    rows, rank_max, strips = u_far.shape
    sides = near_field.shape[0]
    return pl.pallas_call(
        far_kernel,
        in_specs=[VMEM, VMEM, VMEM, VMEM],
        out_specs=VMEM,
        out_shape=jax.ShapeDtypeStruct((sides, rows), f32),
        scratch_shapes=[pltpu.VMEM((rank_max, rows, strips), bf16)],
        compiler_params=pltpu.CompilerParams(vmem_limit_bytes=16 * MiB),
        cost_estimate=pl.CostEstimate(
            flops=2 * rows * rank_max * strips * sides,
            bytes_accessed=2 * rows * rank_max * strips,
            transcendentals=0,
        ),
        name="add_far",
    )(near_field, rank, u_far, coefficients)


def exchanges(strips):
    pairs = strips // 2
    sibling = [(d, d ^ 1) for d in range(strips)]
    first = [(2 * c + 2, 2 * c) for c in range(pairs - 1)] + [(0, 1)]
    first += [(2 * c + 1, 2 * c + 3) for c in range(pairs - 1)] + [(strips - 1, strips - 2)]
    second = [(b, a) for a, b in first]
    groups = [(2 * (c + 3), 2 * c) for c in range(pairs - 3)]
    groups += [(2 * c + 1, 2 * (c + 3) + 1) for c in range(pairs - 3)]
    groups += [(2, 5), (4, 3), (0, 1)]
    groups += [(strips - 1 - a, strips - 1 - b) for a, b in ((2, 5), (4, 3), (0, 1))]
    return sibling, first, second, groups


def body(density, near_blocks, u_far, v_far, ranks, near_list, near_count):
    me = lax.axis_index("strip").astype(jnp.int32).reshape(1)
    sibling, first, second, groups = exchanges(lax.axis_size("strip"))
    source = density.T
    held = [lax.ppermute(source, "strip", moves) for moves in (sibling, first, second)]
    raw, source_bf = project(source, jnp.transpose(v_far, (0, 2, 1)))
    raw, *held[1:] = lax.optimization_barrier((raw, *held[1:]))
    held += [lax.ppermute(strip, "strip", sibling) for strip in held[1:]]
    own = group(me, source_bf, *held)
    raw, own = lax.optimization_barrier((raw, own))
    direct = lax.ppermute(own, "strip", groups)
    outgoing = order(raw)
    incoming = lax.all_to_all(outgoing, "strip", split_axis=0, concat_axis=0, tiled=True)
    swapped = lax.ppermute(direct, "strip", sibling)
    near_field, rank = near(me, near_list, near_count, near_blocks, ranks, own, direct, swapped)
    return add_far(near_field, rank, jnp.transpose(u_far, (0, 2, 1)), incoming).T


def solution(mesh):
    return jax.shard_map(
        body,
        mesh=mesh,
        in_specs=(
            P("strip", None),
            P("strip", None),
            P("strip", None, None),
            P("strip", None, None),
            P(),
            P(),
            P(),
        ),
        out_specs=P("strip", None),
        check_vma=False,
    )
```

```python
import jax
import jax.numpy as jnp
from jax import lax
from jax.experimental import pallas as pl
from jax.experimental.pallas import tpu as pltpu
from jax.sharding import PartitionSpec as P

GROUP = 6

bf16 = jnp.bfloat16
f32 = jnp.float32
MiB = 2**20

SMEM = pl.BlockSpec(memory_space=pltpu.SMEM)
VMEM = pl.BlockSpec(memory_space=pltpu.VMEM)
HBM = pl.BlockSpec(memory_space=pltpu.HBM)


def start_all(copies):
    for copy in copies:
        copy.start()


def project_kernel(pair_ref, v_hbm, out_ref, raw_ref, turned_ref, sems):
    rank_max, rows, strips = turned_ref.shape
    sides = pair_ref.shape[1]
    parts, pieces = sems.shape
    half = rank_max // parts
    chunk = rows // pieces
    copies = staged_copies(v_hbm, raw_ref, sems)
    start_all(copies)
    source = pair_ref[0]
    for h in range(parts):
        for n in range(pieces):
            copies[h * pieces + n].wait()
            turned_ref[pl.ds(h * half, half), pl.ds(n * chunk, chunk), :] = jnp.swapaxes(
                raw_ref[h, pl.ds(n * chunk, chunk)], 0, 1
            )
        factors = jnp.concatenate([turned_ref[h * half + k] for k in range(half)], axis=1)
        product = jnp.dot(source, factors, preferred_element_type=f32)
        for k in range(half):
            place = pl.ds(k % 2 * sides, sides)
            value = product[:, k * strips : (k + 1) * strips]
            out_ref[(h * half + k) // 2, place, :] = value.astype(bf16)


def project(pair, v_far):
    rows, rank_max, strips = v_far.shape
    sides = pair.shape[1]
    parts = 2
    return pl.pallas_call(
        project_kernel,
        in_specs=[VMEM, HBM],
        out_specs=VMEM,
        out_shape=jax.ShapeDtypeStruct((rank_max // 2, 2 * sides, strips), bf16),
        scratch_shapes=[
            pltpu.VMEM((parts, rows, rank_max // parts, strips), bf16),
            pltpu.VMEM((rank_max, rows, strips), bf16),
            pltpu.SemaphoreType.DMA((parts, 4)),
        ],
        compiler_params=pltpu.CompilerParams(vmem_limit_bytes=53 * MiB),
        cost_estimate=pl.CostEstimate(
            flops=2 * rows * rank_max * strips * sides,
            bytes_accessed=2 * rows * rank_max * strips,
            transcendentals=0,
        ),
        name="project",
    )(pair, v_far)


def order_kernel(raw_ref, out_ref):
    turned = jnp.stack([raw_ref[p].T for p in range(raw_ref.shape[0])])
    out_ref[...] = jnp.swapaxes(turned, 0, 1)


def order(raw):
    pairs, width, strips = raw.shape
    return pl.pallas_call(
        order_kernel,
        in_specs=[VMEM],
        out_specs=VMEM,
        out_shape=jax.ShapeDtypeStruct((strips, pairs, width), bf16),
        compiler_params=pltpu.CompilerParams(vmem_limit_bytes=4 * MiB),
        cost_estimate=pl.CostEstimate(
            flops=0, bytes_accessed=4 * pairs * width * strips, transcendentals=0
        ),
        name="order",
    )(raw)


def staged_copies(source_hbm, raw_ref, sems):
    half = raw_ref.shape[2]
    parts, pieces = sems.shape
    chunk = raw_ref.shape[1] // pieces
    return [
        pltpu.make_async_copy(
            source_hbm.at[pl.ds(n * chunk, chunk), pl.ds(h * half, half)],
            raw_ref.at[h, pl.ds(n * chunk, chunk)],
            sems.at[h, n],
        )
        for h in range(parts)
        for n in range(pieces)
    ]


def cast_kernel(in_ref, out_ref):
    out_ref[...] = in_ref[...].astype(bf16)


def cast(value):
    return pl.pallas_call(
        cast_kernel,
        in_specs=[VMEM],
        out_specs=VMEM,
        out_shape=jax.ShapeDtypeStruct(value.shape, bf16),
        compiler_params=pltpu.CompilerParams(vmem_limit_bytes=2 * MiB),
        name="cast",
    )(value)


def pack_kernel(own_ref, sibling_ref, out_ref):
    out_ref[0] = own_ref[...]
    out_ref[1] = sibling_ref[...].astype(bf16)


def pack(own, sibling):
    return pl.pallas_call(
        pack_kernel,
        in_specs=[VMEM, VMEM],
        out_specs=VMEM,
        out_shape=jax.ShapeDtypeStruct((2, *own.shape), bf16),
        compiler_params=pltpu.CompilerParams(vmem_limit_bytes=2 * MiB),
        name="pack",
    )(own, sibling)


def group_kernel(me_ref, pair_ref, next_ref, other_ref, out_ref):
    core = me_ref[0] % 2
    for n in range(2):
        out_ref[2 + (core + n) % 2] = pair_ref[n]
        out_ref[4 - 4 * core + (core + n) % 2] = next_ref[n]
        out_ref[4 * core + (1 - core + n) % 2] = other_ref[n]


def group(me, pair, following, other):
    return pl.pallas_call(
        group_kernel,
        in_specs=[SMEM] + [VMEM] * 3,
        out_specs=VMEM,
        out_shape=jax.ShapeDtypeStruct((GROUP, *pair.shape[1:]), bf16),
        compiler_params=pltpu.CompilerParams(vmem_limit_bytes=4 * MiB),
        name="group",
    )(me, pair, following, other)


def near_kernel(me_ref, list_ref, count_ref, blocks_hbm, ranks_ref, own_ref, direct_ref, swapped_ref, out_ref, rank_ref, table_ref, gathered_ref, tiles_ref, sems):
    slots = list_ref.shape[0]
    parts, chunk, columns = tiles_ref.shape
    rows = columns // slots
    copies = [
        pltpu.make_async_copy(blocks_hbm.at[pl.ds(n * chunk, chunk)], tiles_ref.at[n], sems.at[n])
        for n in range(parts)
    ]
    start_all(copies)
    me = me_ref[0]
    core = me % 2
    strips, width = rank_ref.shape
    hot = (lax.broadcasted_iota(jnp.int32, (strips, width), 0) == me).astype(bf16)
    rank = lax.dot_general(
        ranks_ref[...].astype(f32).astype(bf16),
        hot,
        (((0,), (0,)), ((), ())),
        preferred_element_type=f32,
    )
    odd = lax.broadcasted_iota(jnp.int32, (strips, width), 1) >= out_ref.shape[0]
    rank_ref[...] = (rank - odd.astype(f32)).astype(bf16)
    table_ref[pl.ds(GROUP, GROUP)] = own_ref[...]
    table_ref[pl.ds(2 * GROUP * (1 - core), GROUP)] = direct_ref[...]
    table_ref[pl.ds(2 * GROUP * core, GROUP)] = swapped_ref[...]
    pair = me // 2
    above = jnp.where(pair == list_ref.shape[1] // 2 - 3, pair + 1, pair + 3)
    below = jnp.where(pair == 2, 1, pair - 3)
    for s in range(slots):
        strip = list_ref[s, me]
        side = strip // 2 - pair
        middle = jnp.where(side > 1, above, jnp.where(side < -1, below, pair))
        start = jnp.where(side > 1, 2 * GROUP, jnp.where(side < -1, 0, GROUP))
        place = start + jnp.clip(strip - 2 * (middle - 1), 0, GROUP - 1)
        value = table_ref[place]
        value = jnp.where(s < count_ref[me], value, jnp.zeros_like(value))
        gathered_ref[pl.ds(s * rows, rows), :] = value.T
    for n in range(parts):
        copies[n].wait()
        total = jnp.zeros((2 * chunk, out_ref.shape[0]), f32)
        for s in range(slots):
            tile = tiles_ref[n, :, pl.ds(s * rows, rows)]
            high = tile.astype(bf16)
            low = (tile - high.astype(f32)).astype(bf16)
            total += jnp.dot(
                jnp.concatenate([high, low], axis=0),
                gathered_ref[pl.ds(s * rows, rows), :],
                preferred_element_type=f32,
            )
        out_ref[:, pl.ds(n * chunk, chunk)] = (total[:chunk] + total[chunk:]).T


def near(me, near_list, near_count, near_blocks, ranks, own, direct, swapped):
    rows, columns = near_blocks.shape
    sides = own.shape[1]
    parts = 4
    return pl.pallas_call(
        near_kernel,
        in_specs=[SMEM, SMEM, SMEM, HBM, VMEM, VMEM, VMEM, VMEM],
        out_specs=[VMEM, VMEM],
        out_shape=[
            jax.ShapeDtypeStruct((sides, rows), f32),
            jax.ShapeDtypeStruct((ranks.shape[0], 2 * sides), bf16),
        ],
        scratch_shapes=[
            pltpu.VMEM((3 * GROUP, sides, rows), bf16),
            pltpu.VMEM((columns, sides), bf16),
            pltpu.VMEM((parts, rows // parts, columns), f32),
            pltpu.SemaphoreType.DMA((parts,)),
        ],
        compiler_params=pltpu.CompilerParams(vmem_limit_bytes=52 * MiB),
        cost_estimate=pl.CostEstimate(
            flops=4 * rows * columns * sides,
            bytes_accessed=4 * rows * columns,
            transcendentals=0,
        ),
        name="near",
    )(me, near_list.T, near_count, near_blocks, ranks, own, direct, swapped)


def far_kernel(near_ref, rank_ref, u_hbm, coefficients_ref, out_ref, raw_ref, turned_ref, sems):
    parts, rows, half, strips = raw_ref.shape
    sides = out_ref.shape[0]
    pieces = sems.shape[1]
    chunk = rows // pieces
    copies = staged_copies(u_hbm, raw_ref, sems)
    start_all(copies)
    rank = rank_ref[...]
    turned = jnp.swapaxes(coefficients_ref[...], 0, 1)
    weights = []
    for p in range(parts * half // 2):
        kept = jnp.where(rank > 2 * p, turned[p], jnp.zeros_like(turned[p]))
        weights += [kept[:, :sides], kept[:, sides:]]
    far = jnp.zeros((rows, sides), f32)
    for h in range(parts):
        for n in range(pieces):
            copies[h * pieces + n].wait()
            part = pl.ds(n * chunk, chunk)
            turned_ref[h, :, part, :] = jnp.swapaxes(raw_ref[h, part], 0, 1)
        factors = jnp.concatenate([turned_ref[h, k] for k in range(half)], axis=1)
        part = jnp.concatenate(weights[h * half : (h + 1) * half], axis=0)
        far += jnp.dot(factors, part, preferred_element_type=f32)
    out_ref[...] = near_ref[...] + far.T


def add_far(near_field, rank, u_far, coefficients):
    rows, rank_max, strips = u_far.shape
    sides = near_field.shape[0]
    parts = 2
    half = rank_max // parts
    return pl.pallas_call(
        far_kernel,
        in_specs=[VMEM, VMEM, HBM, VMEM],
        out_specs=VMEM,
        out_shape=jax.ShapeDtypeStruct((sides, rows), f32),
        scratch_shapes=[
            pltpu.VMEM((parts, rows, half, strips), bf16),
            pltpu.VMEM((parts, half, rows, strips), bf16),
            pltpu.SemaphoreType.DMA((parts, 4)),
        ],
        compiler_params=pltpu.CompilerParams(vmem_limit_bytes=53 * MiB),
        cost_estimate=pl.CostEstimate(
            flops=2 * rows * rank_max * strips * sides,
            bytes_accessed=2 * rows * rank_max * strips,
            transcendentals=0,
        ),
        name="add_far",
    )(near_field, rank, u_far, coefficients)


def exchanges(strips):
    pairs = strips // 2
    sibling = [(d, d ^ 1) for d in range(strips)]
    following = [(2 * c + 2, 2 * c) for c in range(pairs - 1)] + [(0, 1)]
    following += [(2 * c + 1, 2 * c + 3) for c in range(pairs - 1)] + [(strips - 1, strips - 2)]
    groups = [(2 * (c + 3), 2 * c) for c in range(pairs - 3)]
    groups += [(2 * c + 1, 2 * (c + 3) + 1) for c in range(pairs - 3)]
    groups += [(2, 5), (4, 3), (0, 1)]
    groups += [(strips - 1 - a, strips - 1 - b) for a, b in ((2, 5), (4, 3), (0, 1))]
    return sibling, following, groups


def body(density, near_blocks, u_far, v_far, ranks, near_list, near_count):
    me = lax.axis_index("strip").astype(jnp.int32).reshape(1)
    sibling, following, groups = exchanges(lax.axis_size("strip"))
    source = density.T
    pair = pack(cast(source), lax.ppermute(source, "strip", sibling))
    follower = lax.ppermute(pair, "strip", following)
    raw = project(pair, jnp.transpose(v_far, (0, 2, 1)))
    raw, follower = lax.optimization_barrier((raw, follower))
    other = lax.ppermute(follower, "strip", sibling)
    outgoing = order(raw)
    outgoing, pair, follower, other = lax.optimization_barrier((outgoing, pair, follower, other))
    own = group(me, pair, follower, other)
    direct = lax.ppermute(own, "strip", groups)
    incoming = lax.all_to_all(outgoing, "strip", split_axis=0, concat_axis=0, tiled=True)
    swapped = lax.ppermute(direct, "strip", sibling)
    near_field, rank = near(me, near_list, near_count, near_blocks, ranks, own, direct, swapped)
    return add_far(near_field, rank, jnp.transpose(u_far, (0, 2, 1)), incoming).T


def solution(mesh):
    return jax.shard_map(
        body,
        mesh=mesh,
        in_specs=(
            P("strip", None),
            P("strip", None),
            P("strip", None, None),
            P("strip", None, None),
            P(),
            P(),
            P(),
        ),
        out_specs=P("strip", None),
        check_vma=False,
    )
```

```python
import jax
import jax.numpy as jnp
from jax import lax
from jax.experimental import pallas as pl
from jax.experimental.pallas import tpu as pltpu
from jax.sharding import PartitionSpec as P

GROUP = 6

bf16 = jnp.bfloat16
f32 = jnp.float32
MiB = 2**20

SMEM = pl.BlockSpec(memory_space=pltpu.SMEM)
VMEM = pl.BlockSpec(memory_space=pltpu.VMEM)
HBM = pl.BlockSpec(memory_space=pltpu.HBM)


def start_all(copies):
    for copy in copies:
        copy.start()


def project_kernel(pair_ref, v_hbm, out_ref, raw_ref, turned_ref, sems):
    rank_max, rows, strips = turned_ref.shape
    sides = pair_ref.shape[1]
    parts, pieces = sems.shape
    half = rank_max // parts
    chunk = rows // pieces
    copies = staged_copies(v_hbm, raw_ref, sems)
    start_all(copies)
    source = pair_ref[0]
    for h in range(parts):
        for n in range(pieces):
            copies[h * pieces + n].wait()
            turned_ref[pl.ds(h * half, half), pl.ds(n * chunk, chunk), :] = jnp.swapaxes(
                raw_ref[h, pl.ds(n * chunk, chunk)], 0, 1
            )
        factors = jnp.concatenate([turned_ref[h * half + k] for k in range(half)], axis=1)
        product = jnp.dot(source, factors, preferred_element_type=f32)
        for k in range(half):
            place = pl.ds(k % 2 * sides, sides)
            value = product[:, k * strips : (k + 1) * strips]
            out_ref[(h * half + k) // 2, place, :] = value.astype(bf16)


def project(pair, v_far):
    rows, rank_max, strips = v_far.shape
    sides = pair.shape[1]
    parts = 2
    return pl.pallas_call(
        project_kernel,
        in_specs=[VMEM, HBM],
        out_specs=VMEM,
        out_shape=jax.ShapeDtypeStruct((rank_max // 2, 2 * sides, strips), bf16),
        scratch_shapes=[
            pltpu.VMEM((parts, rows, rank_max // parts, strips), bf16),
            pltpu.VMEM((rank_max, rows, strips), bf16),
            pltpu.SemaphoreType.DMA((parts, 4)),
        ],
        compiler_params=pltpu.CompilerParams(vmem_limit_bytes=53 * MiB),
        cost_estimate=pl.CostEstimate(
            flops=2 * rows * rank_max * strips * sides,
            bytes_accessed=2 * rows * rank_max * strips,
            transcendentals=0,
        ),
        name="project",
    )(pair, v_far)


def order_kernel(raw_ref, out_ref):
    turned = jnp.stack([raw_ref[p].T for p in range(raw_ref.shape[0])])
    out_ref[...] = jnp.swapaxes(turned, 0, 1)


def order(raw):
    pairs, width, strips = raw.shape
    return pl.pallas_call(
        order_kernel,
        in_specs=[VMEM],
        out_specs=VMEM,
        out_shape=jax.ShapeDtypeStruct((strips, pairs, width), bf16),
        compiler_params=pltpu.CompilerParams(vmem_limit_bytes=4 * MiB),
        cost_estimate=pl.CostEstimate(
            flops=0, bytes_accessed=4 * pairs * width * strips, transcendentals=0
        ),
        name="order",
    )(raw)


def staged_copies(source_hbm, raw_ref, sems):
    half = raw_ref.shape[2]
    parts, pieces = sems.shape
    chunk = raw_ref.shape[1] // pieces
    return [
        pltpu.make_async_copy(
            source_hbm.at[pl.ds(n * chunk, chunk), pl.ds(h * half, half)],
            raw_ref.at[h, pl.ds(n * chunk, chunk)],
            sems.at[h, n],
        )
        for h in range(parts)
        for n in range(pieces)
    ]


def cast_kernel(in_ref, out_ref):
    out_ref[...] = in_ref[...].astype(bf16)


def cast(value):
    return pl.pallas_call(
        cast_kernel,
        in_specs=[VMEM],
        out_specs=VMEM,
        out_shape=jax.ShapeDtypeStruct(value.shape, bf16),
        compiler_params=pltpu.CompilerParams(vmem_limit_bytes=2 * MiB),
        name="cast",
    )(value)


def pack_kernel(own_ref, sibling_ref, out_ref):
    out_ref[0] = own_ref[...]
    out_ref[1] = sibling_ref[...].astype(bf16)


def pack(own, sibling):
    return pl.pallas_call(
        pack_kernel,
        in_specs=[VMEM, VMEM],
        out_specs=VMEM,
        out_shape=jax.ShapeDtypeStruct((2, *own.shape), bf16),
        compiler_params=pltpu.CompilerParams(vmem_limit_bytes=2 * MiB),
        name="pack",
    )(own, sibling)


def group_kernel(me_ref, pair_ref, next_ref, other_ref, out_ref):
    core = me_ref[0] % 2
    for n in range(2):
        out_ref[2 + (core + n) % 2] = pair_ref[n]
        out_ref[4 - 4 * core + (core + n) % 2] = next_ref[n]
        out_ref[4 * core + (1 - core + n) % 2] = other_ref[n]


def group(me, pair, following, other):
    return pl.pallas_call(
        group_kernel,
        in_specs=[SMEM] + [VMEM] * 3,
        out_specs=VMEM,
        out_shape=jax.ShapeDtypeStruct((GROUP, *pair.shape[1:]), bf16),
        compiler_params=pltpu.CompilerParams(vmem_limit_bytes=4 * MiB),
        name="group",
    )(me, pair, following, other)


def near_kernel(me_ref, list_ref, count_ref, blocks_hbm, ranks_ref, own_ref, direct_ref, swapped_ref, out_ref, rank_ref, table_ref, gathered_ref, tiles_ref, sems):
    slots = list_ref.shape[0]
    parts, chunk, columns = tiles_ref.shape
    rows = columns // slots
    copies = [
        pltpu.make_async_copy(blocks_hbm.at[pl.ds(n * chunk, chunk)], tiles_ref.at[n], sems.at[n])
        for n in range(parts)
    ]
    start_all(copies)
    me = me_ref[0]
    core = me % 2
    strips, width = rank_ref.shape
    hot = (lax.broadcasted_iota(jnp.int32, (strips, width), 0) == me).astype(bf16)
    rank = lax.dot_general(
        ranks_ref[...].astype(f32).astype(bf16),
        hot,
        (((0,), (0,)), ((), ())),
        preferred_element_type=f32,
    )
    odd = lax.broadcasted_iota(jnp.int32, (strips, width), 1) >= out_ref.shape[0]
    rank_ref[...] = (rank - odd.astype(f32)).astype(bf16)
    table_ref[pl.ds(GROUP, GROUP)] = own_ref[...]
    table_ref[pl.ds(2 * GROUP * (1 - core), GROUP)] = direct_ref[...]
    table_ref[pl.ds(2 * GROUP * core, GROUP)] = swapped_ref[...]
    pair = me // 2
    above = jnp.where(pair == list_ref.shape[1] // 2 - 3, pair + 1, pair + 3)
    below = jnp.where(pair == 2, 1, pair - 3)
    for s in range(slots):
        strip = list_ref[s, me]
        side = strip // 2 - pair
        middle = jnp.where(side > 1, above, jnp.where(side < -1, below, pair))
        start = jnp.where(side > 1, 2 * GROUP, jnp.where(side < -1, 0, GROUP))
        place = start + jnp.clip(strip - 2 * (middle - 1), 0, GROUP - 1)
        value = table_ref[place]
        value = jnp.where(s < count_ref[me], value, jnp.zeros_like(value))
        gathered_ref[pl.ds(s * rows, rows), :] = value.T
    for n in range(parts):
        copies[n].wait()
        total = jnp.zeros((2 * chunk, out_ref.shape[0]), f32)
        for s in range(slots):
            tile = tiles_ref[n, :, pl.ds(s * rows, rows)]
            high = tile.astype(bf16)
            low = (tile - high.astype(f32)).astype(bf16)
            total += jnp.dot(
                jnp.concatenate([high, low], axis=0),
                gathered_ref[pl.ds(s * rows, rows), :],
                preferred_element_type=f32,
            )
        out_ref[:, pl.ds(n * chunk, chunk)] = (total[:chunk] + total[chunk:]).T


def near(me, near_list, near_count, near_blocks, ranks, own, direct, swapped):
    rows, columns = near_blocks.shape
    sides = own.shape[1]
    parts = 4
    return pl.pallas_call(
        near_kernel,
        in_specs=[SMEM, SMEM, SMEM, HBM, VMEM, VMEM, VMEM, VMEM],
        out_specs=[VMEM, VMEM],
        out_shape=[
            jax.ShapeDtypeStruct((sides, rows), f32),
            jax.ShapeDtypeStruct((ranks.shape[0], 2 * sides), bf16),
        ],
        scratch_shapes=[
            pltpu.VMEM((3 * GROUP, sides, rows), bf16),
            pltpu.VMEM((columns, sides), bf16),
            pltpu.VMEM((parts, rows // parts, columns), f32),
            pltpu.SemaphoreType.DMA((parts,)),
        ],
        compiler_params=pltpu.CompilerParams(vmem_limit_bytes=52 * MiB),
        cost_estimate=pl.CostEstimate(
            flops=4 * rows * columns * sides,
            bytes_accessed=4 * rows * columns,
            transcendentals=0,
        ),
        name="near",
    )(me, near_list.T, near_count, near_blocks, ranks, own, direct, swapped)


def turn_kernel(raw_ref, out_ref):
    out_ref[...] = jnp.swapaxes(raw_ref[...], 0, 1)


def turn_half(factors):
    rows, rank_max, strips = factors.shape
    half = rank_max // 2
    return pl.pallas_call(
        turn_kernel,
        grid=(1,),
        in_specs=[pl.BlockSpec((rows, half, strips), lambda i: (0, 0, 0))],
        out_specs=pl.BlockSpec((half, rows, strips), lambda i: (0, 0, 0)),
        out_shape=jax.ShapeDtypeStruct((half, rows, strips), bf16),
        compiler_params=pltpu.CompilerParams(vmem_limit_bytes=16 * MiB),
        cost_estimate=pl.CostEstimate(
            flops=0, bytes_accessed=2 * rows * rank_max * strips, transcendentals=0
        ),
        name="turn",
    )(factors)


def far_kernel(near_ref, rank_ref, first_ref, u_hbm, coefficients_ref, out_ref, raw_ref, turned_ref, sems):
    half, rows, strips = first_ref.shape
    sides = out_ref.shape[0]
    pieces = sems.shape[0]
    chunk = rows // pieces
    copies = [
        pltpu.make_async_copy(
            u_hbm.at[pl.ds(n * chunk, chunk), pl.ds(half, half)],
            raw_ref.at[pl.ds(n * chunk, chunk)],
            sems.at[n],
        )
        for n in range(pieces)
    ]
    start_all(copies)
    rank = rank_ref[...]
    turned = jnp.swapaxes(coefficients_ref[...], 0, 1)
    weights = []
    for p in range(half):
        kept = jnp.where(rank > 2 * p, turned[p], jnp.zeros_like(turned[p]))
        weights += [kept[:, :sides], kept[:, sides:]]
    factors = jnp.concatenate([first_ref[k] for k in range(half)], axis=1)
    part = jnp.concatenate(weights[:half], axis=0)
    far = jnp.dot(factors, part, preferred_element_type=f32)
    for n in range(pieces):
        copies[n].wait()
        part = pl.ds(n * chunk, chunk)
        turned_ref[:, part, :] = jnp.swapaxes(raw_ref[part], 0, 1)
    factors = jnp.concatenate([turned_ref[k] for k in range(half)], axis=1)
    part = jnp.concatenate(weights[half:], axis=0)
    far += jnp.dot(factors, part, preferred_element_type=f32)
    out_ref[...] = near_ref[...] + far.T


def add_far(near_field, rank, first, u_far, coefficients):
    rows, rank_max, strips = u_far.shape
    sides = near_field.shape[0]
    half = rank_max // 2
    return pl.pallas_call(
        far_kernel,
        in_specs=[VMEM, VMEM, VMEM, HBM, VMEM],
        out_specs=VMEM,
        out_shape=jax.ShapeDtypeStruct((sides, rows), f32),
        scratch_shapes=[
            pltpu.VMEM((rows, half, strips), bf16),
            pltpu.VMEM((half, rows, strips), bf16),
            pltpu.SemaphoreType.DMA((8,)),
        ],
        compiler_params=pltpu.CompilerParams(vmem_limit_bytes=51 * MiB),
        cost_estimate=pl.CostEstimate(
            flops=2 * rows * rank_max * strips * sides,
            bytes_accessed=2 * rows * rank_max * strips,
            transcendentals=0,
        ),
        name="add_far",
    )(near_field, rank, first, u_far, coefficients)


def exchanges(strips):
    pairs = strips // 2
    sibling = [(d, d ^ 1) for d in range(strips)]
    following = [(2 * c + 2, 2 * c) for c in range(pairs - 1)] + [(0, 1)]
    following += [(2 * c + 1, 2 * c + 3) for c in range(pairs - 1)] + [(strips - 1, strips - 2)]
    groups = [(2 * (c + 3), 2 * c) for c in range(pairs - 3)]
    groups += [(2 * c + 1, 2 * (c + 3) + 1) for c in range(pairs - 3)]
    groups += [(2, 5), (4, 3), (0, 1)]
    groups += [(strips - 1 - a, strips - 1 - b) for a, b in ((2, 5), (4, 3), (0, 1))]
    return sibling, following, groups


def body(density, near_blocks, u_far, v_far, ranks, near_list, near_count):
    me = lax.axis_index("strip").astype(jnp.int32).reshape(1)
    sibling, following, groups = exchanges(lax.axis_size("strip"))
    source = density.T
    pair = pack(cast(source), lax.ppermute(source, "strip", sibling))
    follower = lax.ppermute(pair, "strip", following)
    raw = project(pair, jnp.transpose(v_far, (0, 2, 1)))
    raw, follower = lax.optimization_barrier((raw, follower))
    other = lax.ppermute(follower, "strip", sibling)
    outgoing = order(raw)
    outgoing, pair, follower, other = lax.optimization_barrier((outgoing, pair, follower, other))
    own = group(me, pair, follower, other)
    direct = lax.ppermute(own, "strip", groups)
    incoming = lax.all_to_all(outgoing, "strip", split_axis=0, concat_axis=0, tiled=True)
    swapped = lax.ppermute(direct, "strip", sibling)
    near_field, rank = near(me, near_list, near_count, near_blocks, ranks, own, direct, swapped)
    u_far, near_field = lax.optimization_barrier((jnp.transpose(u_far, (0, 2, 1)), near_field))
    return add_far(near_field, rank, turn_half(u_far), u_far, incoming).T


def solution(mesh):
    return jax.shard_map(
        body,
        mesh=mesh,
        in_specs=(
            P("strip", None),
            P("strip", None),
            P("strip", None, None),
            P("strip", None, None),
            P(),
            P(),
            P(),
        ),
        out_specs=P("strip", None),
        check_vma=False,
    )
```

```python
import jax
import jax.numpy as jnp
from jax import lax
from jax.experimental import pallas as pl
from jax.experimental.pallas import tpu as pltpu
from jax.sharding import PartitionSpec as P

GROUP = 6

bf16 = jnp.bfloat16
f32 = jnp.float32
MiB = 2**20

SMEM = pl.BlockSpec(memory_space=pltpu.SMEM)
VMEM = pl.BlockSpec(memory_space=pltpu.VMEM)
HBM = pl.BlockSpec(memory_space=pltpu.HBM)


def start_all(copies):
    for copy in copies:
        copy.start()


def project_kernel(pair_ref, v_hbm, out_ref, raw_ref, turned_ref, sems):
    rank_max, rows, strips = turned_ref.shape
    sides = pair_ref.shape[1]
    parts, pieces = sems.shape
    half = rank_max // parts
    chunk = rows // pieces
    copies = staged_copies(v_hbm, raw_ref, sems)
    start_all(copies)
    source = pair_ref[0]
    for h in range(parts):
        for n in range(pieces):
            copies[h * pieces + n].wait()
            turned_ref[pl.ds(h * half, half), pl.ds(n * chunk, chunk), :] = jnp.swapaxes(
                raw_ref[h, pl.ds(n * chunk, chunk)], 0, 1
            )
        factors = jnp.concatenate([turned_ref[h * half + k] for k in range(half)], axis=1)
        product = jnp.dot(source, factors, preferred_element_type=f32)
        for k in range(half):
            place = pl.ds(k % 2 * sides, sides)
            value = product[:, k * strips : (k + 1) * strips]
            out_ref[(h * half + k) // 2, place, :] = value.astype(bf16)


def project(pair, v_far):
    rows, rank_max, strips = v_far.shape
    sides = pair.shape[1]
    parts = 2
    return pl.pallas_call(
        project_kernel,
        in_specs=[VMEM, HBM],
        out_specs=VMEM,
        out_shape=jax.ShapeDtypeStruct((rank_max // 2, 2 * sides, strips), bf16),
        scratch_shapes=[
            pltpu.VMEM((parts, rows, rank_max // parts, strips), bf16),
            pltpu.VMEM((rank_max, rows, strips), bf16),
            pltpu.SemaphoreType.DMA((parts, 8)),
        ],
        compiler_params=pltpu.CompilerParams(vmem_limit_bytes=53 * MiB),
        cost_estimate=pl.CostEstimate(
            flops=2 * rows * rank_max * strips * sides,
            bytes_accessed=2 * rows * rank_max * strips,
            transcendentals=0,
        ),
        name="project",
    )(pair, v_far)


def order_kernel(raw_ref, out_ref):
    turned = jnp.stack([raw_ref[p].T for p in range(raw_ref.shape[0])])
    out_ref[...] = jnp.swapaxes(turned, 0, 1)


def order(raw):
    pairs, width, strips = raw.shape
    return pl.pallas_call(
        order_kernel,
        in_specs=[VMEM],
        out_specs=VMEM,
        out_shape=jax.ShapeDtypeStruct((strips, pairs, width), bf16),
        compiler_params=pltpu.CompilerParams(vmem_limit_bytes=4 * MiB),
        cost_estimate=pl.CostEstimate(
            flops=0, bytes_accessed=4 * pairs * width * strips, transcendentals=0
        ),
        name="order",
    )(raw)


def staged_copies(source_hbm, raw_ref, sems):
    half = raw_ref.shape[2]
    parts, pieces = sems.shape
    chunk = raw_ref.shape[1] // pieces
    return [
        pltpu.make_async_copy(
            source_hbm.at[pl.ds(n * chunk, chunk), pl.ds(h * half, half)],
            raw_ref.at[h, pl.ds(n * chunk, chunk)],
            sems.at[h, n],
        )
        for h in range(parts)
        for n in range(pieces)
    ]


def cast_kernel(in_ref, out_ref):
    out_ref[...] = in_ref[...].astype(bf16)


def cast(value):
    return pl.pallas_call(
        cast_kernel,
        in_specs=[VMEM],
        out_specs=VMEM,
        out_shape=jax.ShapeDtypeStruct(value.shape, bf16),
        compiler_params=pltpu.CompilerParams(vmem_limit_bytes=2 * MiB),
        name="cast",
    )(value)


def pack_kernel(own_ref, sibling_ref, out_ref):
    out_ref[0] = own_ref[...]
    out_ref[1] = sibling_ref[...].astype(bf16)


def pack(own, sibling):
    return pl.pallas_call(
        pack_kernel,
        in_specs=[VMEM, VMEM],
        out_specs=VMEM,
        out_shape=jax.ShapeDtypeStruct((2, *own.shape), bf16),
        compiler_params=pltpu.CompilerParams(vmem_limit_bytes=2 * MiB),
        name="pack",
    )(own, sibling)


def group_kernel(me_ref, pair_ref, next_ref, other_ref, out_ref):
    core = me_ref[0] % 2
    for n in range(2):
        out_ref[2 + (core + n) % 2] = pair_ref[n]
        out_ref[4 - 4 * core + (core + n) % 2] = next_ref[n]
        out_ref[4 * core + (1 - core + n) % 2] = other_ref[n]


def group(me, pair, following, other):
    return pl.pallas_call(
        group_kernel,
        in_specs=[SMEM] + [VMEM] * 3,
        out_specs=VMEM,
        out_shape=jax.ShapeDtypeStruct((GROUP, *pair.shape[1:]), bf16),
        compiler_params=pltpu.CompilerParams(vmem_limit_bytes=4 * MiB),
        name="group",
    )(me, pair, following, other)


def near_kernel(me_ref, list_ref, count_ref, blocks_hbm, ranks_ref, own_ref, direct_ref, swapped_ref, out_ref, rank_ref, table_ref, gathered_ref, tiles_ref, sems):
    slots = list_ref.shape[0]
    parts, chunk, columns = tiles_ref.shape
    rows = columns // slots
    copies = [
        pltpu.make_async_copy(blocks_hbm.at[pl.ds(n * chunk, chunk)], tiles_ref.at[n], sems.at[n])
        for n in range(parts)
    ]
    start_all(copies)
    me = me_ref[0]
    core = me % 2
    strips, width = rank_ref.shape
    hot = (lax.broadcasted_iota(jnp.int32, (strips, width), 0) == me).astype(bf16)
    rank = lax.dot_general(
        ranks_ref[...].astype(f32).astype(bf16),
        hot,
        (((0,), (0,)), ((), ())),
        preferred_element_type=f32,
    )
    odd = lax.broadcasted_iota(jnp.int32, (strips, width), 1) >= out_ref.shape[0]
    rank_ref[...] = (rank - odd.astype(f32)).astype(bf16)
    table_ref[pl.ds(GROUP, GROUP)] = own_ref[...]
    table_ref[pl.ds(2 * GROUP * (1 - core), GROUP)] = direct_ref[...]
    table_ref[pl.ds(2 * GROUP * core, GROUP)] = swapped_ref[...]
    pair = me // 2
    above = jnp.where(pair == list_ref.shape[1] // 2 - 3, pair + 1, pair + 3)
    below = jnp.where(pair == 2, 1, pair - 3)
    for s in range(slots):
        strip = list_ref[s, me]
        side = strip // 2 - pair
        middle = jnp.where(side > 1, above, jnp.where(side < -1, below, pair))
        start = jnp.where(side > 1, 2 * GROUP, jnp.where(side < -1, 0, GROUP))
        place = start + jnp.clip(strip - 2 * (middle - 1), 0, GROUP - 1)
        value = table_ref[place]
        value = jnp.where(s < count_ref[me], value, jnp.zeros_like(value))
        gathered_ref[pl.ds(s * rows, rows), :] = value.T
    for n in range(parts):
        copies[n].wait()
        total = jnp.zeros((2 * chunk, out_ref.shape[0]), f32)
        for s in range(slots):
            tile = tiles_ref[n, :, pl.ds(s * rows, rows)]
            high = tile.astype(bf16)
            low = (tile - high.astype(f32)).astype(bf16)
            total += jnp.dot(
                jnp.concatenate([high, low], axis=0),
                gathered_ref[pl.ds(s * rows, rows), :],
                preferred_element_type=f32,
            )
        out_ref[:, pl.ds(n * chunk, chunk)] = (total[:chunk] + total[chunk:]).T


def near(me, near_list, near_count, near_blocks, ranks, own, direct, swapped):
    rows, columns = near_blocks.shape
    sides = own.shape[1]
    parts = 4
    return pl.pallas_call(
        near_kernel,
        in_specs=[SMEM, SMEM, SMEM, HBM, VMEM, VMEM, VMEM, VMEM],
        out_specs=[VMEM, VMEM],
        out_shape=[
            jax.ShapeDtypeStruct((sides, rows), f32),
            jax.ShapeDtypeStruct((ranks.shape[0], 2 * sides), bf16),
        ],
        scratch_shapes=[
            pltpu.VMEM((3 * GROUP, sides, rows), bf16),
            pltpu.VMEM((columns, sides), bf16),
            pltpu.VMEM((parts, rows // parts, columns), f32),
            pltpu.SemaphoreType.DMA((parts,)),
        ],
        compiler_params=pltpu.CompilerParams(vmem_limit_bytes=52 * MiB),
        cost_estimate=pl.CostEstimate(
            flops=4 * rows * columns * sides,
            bytes_accessed=4 * rows * columns,
            transcendentals=0,
        ),
        name="near",
    )(me, near_list.T, near_count, near_blocks, ranks, own, direct, swapped)


def turn_kernel(raw_ref, out_ref):
    out_ref[...] = jnp.swapaxes(raw_ref[...], 0, 1)


def turn_half(factors):
    rows, rank_max, strips = factors.shape
    half = rank_max // 2
    return pl.pallas_call(
        turn_kernel,
        grid=(1,),
        in_specs=[pl.BlockSpec((rows, half, strips), lambda i: (0, 0, 0))],
        out_specs=pl.BlockSpec((half, rows, strips), lambda i: (0, 0, 0)),
        out_shape=jax.ShapeDtypeStruct((half, rows, strips), bf16),
        compiler_params=pltpu.CompilerParams(vmem_limit_bytes=16 * MiB),
        cost_estimate=pl.CostEstimate(
            flops=0, bytes_accessed=2 * rows * rank_max * strips, transcendentals=0
        ),
        name="turn",
    )(factors)


def far_kernel(near_ref, rank_ref, first_ref, u_hbm, coefficients_ref, out_ref, raw_ref, turned_ref, sems):
    half, rows, strips = first_ref.shape
    sides = out_ref.shape[0]
    pieces = sems.shape[0]
    chunk = rows // pieces
    copies = [
        pltpu.make_async_copy(
            u_hbm.at[pl.ds(n * chunk, chunk), pl.ds(half, half)],
            raw_ref.at[pl.ds(n * chunk, chunk)],
            sems.at[n],
        )
        for n in range(pieces)
    ]
    start_all(copies)
    rank = rank_ref[...]
    turned = jnp.swapaxes(coefficients_ref[...], 0, 1)
    weights = []
    for p in range(half):
        kept = jnp.where(rank > 2 * p, turned[p], jnp.zeros_like(turned[p]))
        weights += [kept[:, :sides], kept[:, sides:]]
    factors = jnp.concatenate([first_ref[k] for k in range(half)], axis=1)
    part = jnp.concatenate(weights[:half], axis=0)
    far = jnp.dot(factors, part, preferred_element_type=f32)
    for n in range(pieces):
        copies[n].wait()
        part = pl.ds(n * chunk, chunk)
        turned_ref[:, part, :] = jnp.swapaxes(raw_ref[part], 0, 1)
    factors = jnp.concatenate([turned_ref[k] for k in range(half)], axis=1)
    part = jnp.concatenate(weights[half:], axis=0)
    far += jnp.dot(factors, part, preferred_element_type=f32)
    out_ref[...] = near_ref[...] + far.T


def add_far(near_field, rank, first, u_far, coefficients):
    rows, rank_max, strips = u_far.shape
    sides = near_field.shape[0]
    half = rank_max // 2
    return pl.pallas_call(
        far_kernel,
        in_specs=[VMEM, VMEM, VMEM, HBM, VMEM],
        out_specs=VMEM,
        out_shape=jax.ShapeDtypeStruct((sides, rows), f32),
        scratch_shapes=[
            pltpu.VMEM((rows, half, strips), bf16),
            pltpu.VMEM((half, rows, strips), bf16),
            pltpu.SemaphoreType.DMA((8,)),
        ],
        compiler_params=pltpu.CompilerParams(vmem_limit_bytes=51 * MiB),
        cost_estimate=pl.CostEstimate(
            flops=2 * rows * rank_max * strips * sides,
            bytes_accessed=2 * rows * rank_max * strips,
            transcendentals=0,
        ),
        name="add_far",
    )(near_field, rank, first, u_far, coefficients)


def exchanges(strips):
    pairs = strips // 2
    sibling = [(d, d ^ 1) for d in range(strips)]
    following = [(2 * c + 2, 2 * c) for c in range(pairs - 1)] + [(0, 1)]
    following += [(2 * c + 1, 2 * c + 3) for c in range(pairs - 1)] + [(strips - 1, strips - 2)]
    groups = [(2 * (c + 3), 2 * c) for c in range(pairs - 3)]
    groups += [(2 * c + 1, 2 * (c + 3) + 1) for c in range(pairs - 3)]
    groups += [(2, 5), (4, 3), (0, 1)]
    groups += [(strips - 1 - a, strips - 1 - b) for a, b in ((2, 5), (4, 3), (0, 1))]
    return sibling, following, groups


def body(density, near_blocks, u_far, v_far, ranks, near_list, near_count):
    me = lax.axis_index("strip").astype(jnp.int32).reshape(1)
    sibling, following, groups = exchanges(lax.axis_size("strip"))
    source = density.T
    pair = pack(cast(source), lax.ppermute(source, "strip", sibling))
    follower = lax.ppermute(pair, "strip", following)
    raw = project(pair, jnp.transpose(v_far, (0, 2, 1)))
    raw, follower = lax.optimization_barrier((raw, follower))
    other = lax.ppermute(follower, "strip", sibling)
    outgoing = order(raw)
    outgoing, pair, follower, other = lax.optimization_barrier((outgoing, pair, follower, other))
    own = group(me, pair, follower, other)
    direct = lax.ppermute(own, "strip", groups)
    incoming = lax.all_to_all(outgoing, "strip", split_axis=0, concat_axis=0, tiled=True)
    swapped = lax.ppermute(direct, "strip", sibling)
    near_field, rank = near(me, near_list, near_count, near_blocks, ranks, own, direct, swapped)
    u_far, near_field = lax.optimization_barrier((jnp.transpose(u_far, (0, 2, 1)), near_field))
    return add_far(near_field, rank, turn_half(u_far), u_far, incoming).T


def solution(mesh):
    return jax.shard_map(
        body,
        mesh=mesh,
        in_specs=(
            P("strip", None),
            P("strip", None),
            P("strip", None, None),
            P("strip", None, None),
            P(),
            P(),
            P(),
        ),
        out_specs=P("strip", None),
        check_vma=False,
    )
```
